32 devices in a mesh: dp: 8 (over y, x, core), tensor: 4 (over z).
Axes of the slice: x: 2, y: 2, z: 4, core: 2. Of those that a mesh axis runs over, the one named last changes fastest.
Arguments:
- inputs: bfloat16 [8192, 8192], P('dp', 'tensor'), may hold values from -6 to 6
- cotangent: bfloat16 [8192, 8192], P('dp', 'tensor'), may hold values from -6 to 6
- projector: bfloat16 [8192, 512], P('tensor'), may hold values from -0.0625 to 0.0625
- weight: bfloat16 [8192, 8192], P('dp', 'tensor'), may hold values from -6 to 6
- moment: float32 [512, 8192], P('dp', 'tensor'), may hold values from -6 to 6
- second_moment: float32 [512, 8192], P('dp', 'tensor'), may hold values from 0.01 to 1
Outputs:
- new_weight: bfloat16 [8192, 8192], P('dp', 'tensor')
- new_moment: float32 [512, 8192], P('dp', 'tensor')
- new_second: float32 [512, 8192], P('dp', 'tensor')
The draws below stay inside these ranges and needn't reach their ends.
All inputs are finite; a program needn't handle non-finite values.
Results may differ from the reference program's by a relative error of at most 0.0034.
Values may be sent and summed in bfloat16 or wider, within the bound.
A program may use at most 64 MiB of HBM per device.

```python
import math
import jax
import jax.numpy as jnp

D = 8192
RANK = 512
STEP = 1000
TOKENS = 8192


def steps_of(own_key, shape, pieces, smallest, top_value):
    level = 1.0
    for dim, blocks in pieces:
        heights = jax.random.uniform(jax.random.fold_in(jax.random.fold_in(own_key, 6), dim), (blocks,), jnp.float32, smallest / len(pieces), top_value / len(pieces))
        level = level * jnp.repeat(jnp.exp(heights), shape[dim] // blocks).reshape((-1,) + (1,) * (len(shape) - 1 - dim))
    return level


def normal_values(own_key, extent, width, limit, shards=(), held_as=jnp.bfloat16):
    array = width * jax.random.normal(own_key, extent, jnp.float32)
    if shards:
        array = array * steps_of(own_key, extent, shards, -0.22, 0.18)
    return jnp.clip(array, -limit, limit).astype(held_as)


def setup_inputs(seed: int = 0) -> dict:
    splits = jax.random.split(jax.random.key(seed), 7)
    return {
        "inputs": normal_values(splits[0], (TOKENS, D), 1.0, 6.0, ((0, 8), (1, 4))),
        "cotangent": normal_values(splits[1], (TOKENS, D), 1.0, 6.0, ((0, 8), (1, 4))),
        "projector": normal_values(splits[2], (D, RANK), D ** -0.5, 0.0625, ((0, 4),)),
        "weight": normal_values(splits[3], (D, D), 1.0, 6.0, ((0, 8), (1, 4))),
        "moment": normal_values(splits[4], (RANK, D), 1.0, 6.0, ((0, 8), (1, 4)), jnp.float32),
        "second_moment": jnp.clip(jnp.exp(math.log(1.0) - 4.6051702 * jax.random.uniform(splits[5], (RANK, D), jnp.float32) ** steps_of(splits[5], (RANK, D), ((0, 8), (1, 4)), -0.2, 0.2)), 0.01, 1.0),
    }


beta_one = 0.9
beta_two = 0.999
epsilon = 1e-08
step_size = 0.5

def reference(inputs, cotangent, projector, weight, moment, second_moment):
    projected = jnp.dot(inputs, projector, preferred_element_type=jnp.float32).astype(jnp.bfloat16)
    gradient = jnp.dot(projected.T, cotangent, preferred_element_type=jnp.float32) * (1.0 / math.sqrt(TOKENS))
    new_moment = beta_one * moment + (1.0 - beta_one) * gradient
    new_second = beta_two * second_moment + (1.0 - beta_two) * gradient * gradient
    first_fix = 1.0 - beta_one ** STEP
    second_fix = 1.0 - beta_two ** STEP
    update = (new_moment / first_fix / (jnp.sqrt(new_second / second_fix) + epsilon)).astype(jnp.bfloat16)
    expanded = jnp.dot(projector, update, preferred_element_type=jnp.float32)
    new_weight = (weight.astype(jnp.float32) - step_size * expanded).astype(jnp.bfloat16)
    return (new_weight, new_moment, new_second)
```

```python
import math

import jax
import jax.numpy as jnp
from jax import lax
from jax.experimental import pallas as pl
from jax.experimental.pallas import tpu as pltpu
from jax.sharding import PartitionSpec as P

STEP = 1000

beta_one = 0.9
beta_two = 0.999
epsilon = 1e-08
step_size = 0.5

TOKEN_CHUNKS = 8
COLUMN_CHUNKS = 4
BASIS_CHUNKS = 8
MESH = pl.DeviceIdType.MESH


def make_kernel(tensor_count, data_count, tokens, features, rank, rows, columns):
    K, NC, NB = TOKEN_CHUNKS, COLUMN_CHUNKS, BASIS_CHUNKS
    tc, w, br = tokens // K, columns // NC, rows // NB
    r = rank // data_count
    m = data_count // 2
    half = tensor_count // 2
    ratio = features // rows
    scale = 1.0 / math.sqrt(tokens * data_count)
    first_fix = 1.0 - beta_one**STEP
    second_fix = 1.0 - beta_two**STEP

    def kernel(
        x_hbm, c_hbm, p_hbm, w_hbm, m_hbm, v_hbm,
        out, new_m, new_v,
        x, cot, proj, wt, mom, sec,
        sfull, zsend, zrecv, exrecv, projd, grad,
        sibsend, sibrecv, own, cssend, csrecv, upd, basis,
        x_sem, l_sem, in_s, in_r, ex_s, ex_r, out_s, out_r,
        sib_s, sib_r, cs_s, cs_r, up_s, up_r, fw_s, fw_r,
        dn_s, dn_r, hi_s, hi_r,
    ):
        t = lax.axis_index("tensor")
        i = lax.axis_index("dp")
        n = tensor_count
        parity = lax.rem(i, 2)
        chip = lax.div(i, 2)
        sibling = i + 1 - 2 * parity
        lower = t < half
        tin = jnp.where(lower, t + 1, t - 1)
        tout = jnp.where(lower, t - 1, t + 1)
        dist = jnp.where(lower, half - 1 - t, t - half)
        is_ex = dist == 0
        has_outer = dist < half - 1
        lag = 1 + 5 * dist
        source = lax.div(i, ratio)
        part = lax.rem(i, ratio)

        def local(k, src, dst):
            return pltpu.make_async_copy(src, dst, l_sem.at[k])

        def xload(k):
            return pltpu.make_async_copy(
                x_hbm.at[pl.ds(k * tc, tc)], x.at[pl.ds(k * tc, tc)], x_sem.at[k]
            )

        loads = [
            local(0, p_hbm, proj),
            local(1, c_hbm, cot),
            local(2, m_hbm, mom),
            local(3, v_hbm, sec),
            local(4, w_hbm, wt),
        ]
        loads[0].start()
        for k in range(K):
            xload(k).start()
        for load in loads[1:]:
            load.start()

        barrier = pltpu.get_barrier_semaphore()

        @pl.when(t > 0)
        def _():
            pl.semaphore_signal(barrier, inc=1, device_id={"tensor": t - 1}, device_id_type=MESH)

        @pl.when(t < n - 1)
        def _():
            pl.semaphore_signal(barrier, inc=1, device_id={"tensor": t + 1}, device_id_type=MESH)

        pl.semaphore_signal(barrier, inc=1, device_id={"dp": sibling}, device_id_type=MESH)
        for d in range(1, m):
            peer = 2 * lax.rem(chip + d, m) + parity
            pl.semaphore_signal(barrier, inc=1, device_id={"dp": peer}, device_id_type=MESH)

        def remote(src, dst, send, recv, where):
            return pltpu.make_async_remote_copy(
                src_ref=src, dst_ref=dst, send_sem=send, recv_sem=recv,
                device_id=where, device_id_type=MESH,
            )

        def inward(k):
            return remote(zsend.at[k], zrecv.at[k], in_s.at[k], in_r.at[k], {"tensor": tin})

        def exchange(k):
            return remote(zsend.at[k], exrecv.at[k], ex_s.at[k], ex_r.at[k], {"tensor": tin})

        def outward(k):
            return remote(projd.at[k], projd.at[k], out_s.at[k], out_r.at[k], {"tensor": tout})

        def basis_down(k):
            return remote(basis.at[k], basis.at[k], dn_s.at[k], dn_r.at[k], {"tensor": t - 1})

        def basis_up(k):
            return remote(basis.at[k], basis.at[k], hi_s.at[k], hi_r.at[k], {"tensor": t + 1})

        def product(k):
            xload(k).wait()
            sfull[k] = jnp.dot(
                x[pl.ds(pl.multiple_of(k * tc, tc), tc), :],
                proj[...],
                preferred_element_type=jnp.float32,
            )

        loads[0].wait()
        product(0)
        grad[...] = jnp.zeros_like(grad)
        pl.semaphore_wait(
            barrier, m + jnp.where(t > 0, 1, 0) + jnp.where(t < n - 1, 1, 0)
        )
        loads[1].wait()

        def reduce_step(k):
            @pl.when(has_outer)
            def _():
                inward(k).wait_recv()
                sfull[k] = sfull[k] + zrecv[k].astype(jnp.float32)

            zsend[k] = sfull[k].astype(jnp.bfloat16)

            @pl.when(is_ex)
            def _():
                exchange(k).start()

            @pl.when(jnp.logical_not(is_ex))
            def _():
                inward(k).start()

        def total_step(k):
            @pl.when(is_ex)
            def _():
                exchange(k).wait_recv()
                projd[k] = (sfull[k] + exrecv[k].astype(jnp.float32)).astype(jnp.bfloat16)

            @pl.when(jnp.logical_not(is_ex))
            def _():
                outward(k).wait_recv()

            @pl.when(has_outer)
            def _():
                outward(k).start()

            def tile(q, carry):
                cols = pl.ds(pl.multiple_of(q * w, w), w)
                grad[:, cols] += lax.dot_general(
                    projd[k],
                    cot[pl.ds(pl.multiple_of(k * tc, tc), tc), cols],
                    (((0,), (0,)), ((), ())),
                    preferred_element_type=jnp.float32,
                )
                return carry

            lax.fori_loop(0, NC, tile, 0)

        def z_step(s, carry):
            @pl.when(s + 1 < K)
            def _():
                product(s + 1)

            @pl.when(s < K)
            def _():
                reduce_step(s)

            @pl.when(jnp.logical_and(s >= lag, s < lag + K))
            def _():
                total_step(s - lag)

            return carry

        lax.fori_loop(0, K + 1 + 5 * (half - 1), z_step, 0)

        @pl.when(t == source)
        def _():
            def send(k, carry):
                basis[k] = proj[pl.ds(pl.multiple_of(part * rows + k * br, br), br), :]

                @pl.when(t > 0)
                def _():
                    basis_down(k).start()

                @pl.when(t < n - 1)
                def _():
                    basis_up(k).start()

                return carry

            lax.fori_loop(0, NB, send, 0)

        def basis_step(k):
            @pl.when(t < source)
            def _():
                basis_down(k).wait_recv()

                @pl.when(t > 0)
                def _():
                    basis_down(k).start()

            @pl.when(t > source)
            def _():
                basis_up(k).wait_recv()

                @pl.when(t < n - 1)
                def _():
                    basis_up(k).start()

        def to_sibling(q):
            return remote(
                sibsend.at[q], sibrecv.at[q], sib_s.at[q], sib_r.at[q], {"dp": sibling}
            )

        def to_chip(q, d):
            peer = 2 * lax.rem(chip + d, m) + parity
            return remote(
                cssend.at[q, d], csrecv.at[q, d], cs_s.at[q, d], cs_r.at[q, d], {"dp": peer}
            )

        def block(owner):
            return pl.ds(pl.multiple_of(owner * r, r), r)

        def update_to_chip(q, d):
            peer = 2 * lax.rem(chip + d, m) + parity
            return remote(
                upd.at[q, block(i)], upd.at[q, block(i)], up_s.at[q, d], up_r.at[q, d],
                {"dp": peer},
            )

        def update_to_sibling(q, d):
            owner = 2 * lax.rem(chip - d + m, m) + parity
            return remote(
                upd.at[q, block(owner)], upd.at[q, block(owner)], fw_s.at[q, d], fw_r.at[q, d],
                {"dp": sibling},
            )

        def sibling_step(q, carry):
            cols = pl.ds(pl.multiple_of(q * w, w), w)
            for j in range(m):
                sibsend[q, j] = grad[block(2 * j + 1 - parity), cols].astype(jnp.bfloat16)
            to_sibling(q).start()
            return carry

        lax.fori_loop(0, NC, sibling_step, 0)

        def chip_step(q, carry):
            cols = pl.ds(pl.multiple_of(q * w, w), w)
            to_sibling(q).wait_recv()
            for d in range(1, m):
                j = lax.rem(chip + d, m)
                cssend[q, d] = (
                    grad[block(2 * j + parity), cols] + sibrecv[q, j].astype(jnp.float32)
                ).astype(jnp.bfloat16)
                to_chip(q, d).start()
            own[q] = grad[block(i), cols] + sibrecv[q, chip].astype(jnp.float32)
            return carry

        lax.fori_loop(0, NC, chip_step, 0)
        loads[2].wait()
        loads[3].wait()

        def adam_step(q, carry):
            cols = pl.ds(pl.multiple_of(q * w, w), w)

            @pl.when(q >= 1)
            def _():
                basis_step(q - 1)

            total = own[q]
            for d in range(1, m):
                to_chip(q, d).wait_recv()
                total = total + csrecv[q, d].astype(jnp.float32)
            gradient = total * scale
            moment = beta_one * mom[:, cols] + (1.0 - beta_one) * gradient
            second = beta_two * sec[:, cols] + (1.0 - beta_two) * gradient * gradient
            new_m[:, cols] = moment
            new_v[:, cols] = second
            upd[q, block(i)] = (
                moment / first_fix / (jnp.sqrt(second / second_fix) + epsilon)
            ).astype(jnp.bfloat16)
            for d in range(1, m):
                update_to_chip(q, d).start()
            update_to_sibling(q, 0).start()
            return carry

        lax.fori_loop(0, NC, adam_step, 0)

        def gather_step(q, carry):
            basis_step(q + NC - 1)
            for d in range(1, m):
                update_to_chip(q, d).wait_recv()
                update_to_sibling(q, d).start()
            return carry

        lax.fori_loop(0, NC, gather_step, 0)
        for k in range(2 * NC - 1, NB):
            basis_step(k)

        loads[4].wait()

        def sibling_wait(q, carry):
            for d in range(m):
                owner = 2 * lax.rem(chip - d + m, m) + 1 - parity
                remote(
                    upd.at[q, block(owner)], upd.at[q, block(owner)],
                    fw_s.at[q, d], fw_r.at[q, d], {"dp": sibling},
                ).wait_recv()
            return carry

        lax.fori_loop(0, NC, sibling_wait, 0)

        def final(q, carry):
            cols = pl.ds(pl.multiple_of(q * w, w), w)

            def row_step(k, carry):
                lines = pl.ds(pl.multiple_of(k * br, br), br)
                expanded = jnp.dot(basis[k], upd[q], preferred_element_type=jnp.float32)
                out[lines, cols] = (
                    wt[lines, cols].astype(jnp.float32) - step_size * expanded
                ).astype(jnp.bfloat16)
                return carry

            return lax.fori_loop(0, NB, row_step, carry)

        lax.fori_loop(0, NC, final, 0)

        def drain_z(k, carry):
            @pl.when(is_ex)
            def _():
                exchange(k).wait_send()

            @pl.when(jnp.logical_not(is_ex))
            def _():
                inward(k).wait_send()

            @pl.when(has_outer)
            def _():
                outward(k).wait_send()

            return carry

        lax.fori_loop(0, K, drain_z, 0)

        def drain_basis(k, carry):
            @pl.when(jnp.logical_and(t <= source, t > 0))
            def _():
                basis_down(k).wait_send()

            @pl.when(jnp.logical_and(t >= source, t < n - 1))
            def _():
                basis_up(k).wait_send()

            return carry

        lax.fori_loop(0, NB, drain_basis, 0)

        def drain_dp(q, carry):
            to_sibling(q).wait_send()
            update_to_sibling(q, 0).wait_send()
            for d in range(1, m):
                to_chip(q, d).wait_send()
                update_to_chip(q, d).wait_send()
                update_to_sibling(q, d).wait_send()
            return carry

        lax.fori_loop(0, NC, drain_dp, 0)

    dma = pltpu.SemaphoreType.DMA
    bf16, f32 = jnp.bfloat16, jnp.float32
    scratch = [
        pltpu.VMEM((tokens, features), bf16),
        pltpu.VMEM((tokens, columns), bf16),
        pltpu.VMEM((features, rank), bf16),
        pltpu.VMEM((rows, columns), bf16),
        pltpu.VMEM((r, columns), f32),
        pltpu.VMEM((r, columns), f32),
        pltpu.VMEM((K, tc, rank), f32),
        pltpu.VMEM((K, tc, rank), bf16),
        pltpu.VMEM((K, tc, rank), bf16),
        pltpu.VMEM((K, tc, rank), bf16),
        pltpu.VMEM((K, tc, rank), bf16),
        pltpu.VMEM((rank, columns), f32),
        pltpu.VMEM((NC, m, r, w), bf16),
        pltpu.VMEM((NC, m, r, w), bf16),
        pltpu.VMEM((NC, r, w), f32),
        pltpu.VMEM((NC, m, r, w), bf16),
        pltpu.VMEM((NC, m, r, w), bf16),
        pltpu.VMEM((NC, rank, w), bf16),
        pltpu.VMEM((NB, br, rank), bf16),
        dma((K,)),
        dma((5,)),
        *[dma((K,))] * 6,
        *[dma((NC,))] * 2,
        *[dma((NC, m))] * 6,
        *[dma((NB,))] * 4,
    ]
    return kernel, scratch


def solution(mesh):
    tensor_count, data_count = mesh.shape["tensor"], mesh.shape["dp"]

    def on_device(inputs, cotangent, projector, weight, moment, second_moment):
        tokens, features = inputs.shape
        rank = projector.shape[1]
        rows, columns = weight.shape
        kernel, scratch = make_kernel(
            tensor_count, data_count, tokens, features, rank, rows, columns
        )
        return pl.pallas_call(
            kernel,
            out_shape=(
                jax.ShapeDtypeStruct(weight.shape, weight.dtype),
                jax.ShapeDtypeStruct(moment.shape, moment.dtype),
                jax.ShapeDtypeStruct(second_moment.shape, second_moment.dtype),
            ),
            in_specs=[pl.BlockSpec(memory_space=pl.ANY)] * 6,
            out_specs=tuple([pl.BlockSpec(memory_space=pltpu.VMEM)] * 3),
            scratch_shapes=scratch,
            compiler_params=pltpu.CompilerParams(
                collective_id=0, has_side_effects=True, vmem_limit_bytes=60 * 1024 * 1024
            ),
        )(inputs, cotangent, projector, weight, moment, second_moment)

    return jax.shard_map(
        on_device,
        mesh=mesh,
        in_specs=(
            P("dp", "tensor"),
            P("dp", "tensor"),
            P("tensor", None),
            P("dp", "tensor"),
            P("dp", "tensor"),
            P("dp", "tensor"),
        ),
        out_specs=(P("dp", "tensor"), P("dp", "tensor"), P("dp", "tensor")),
        check_vma=False,
    )
```

```python
import math

import jax
import jax.numpy as jnp
from jax import lax
from jax.experimental import pallas as pl
from jax.experimental.pallas import tpu as pltpu
from jax.sharding import PartitionSpec as P

STEP = 1000

beta_one = 0.9
beta_two = 0.999
epsilon = 1e-08
step_size = 0.5

TOKEN_CHUNKS = 16
GROUP = 2
LAG = 3
HOP_LAG = 7
COLUMN_CHUNKS = 4
BASIS_CHUNKS = 8
MESH = pl.DeviceIdType.MESH


def make_kernel(tensor_count, data_count, tokens, features, rank, rows, columns):
    K, NC, NB = TOKEN_CHUNKS, COLUMN_CHUNKS, BASIS_CHUNKS
    tc, w, br = tokens // K, columns // NC, rows // NB
    tg = tc * GROUP
    r = rank // data_count
    m = data_count // 2
    half = tensor_count // 2
    ratio = features // rows
    scale = 1.0 / math.sqrt(tokens * data_count)
    first_fix = 1.0 - beta_one**STEP
    second_fix = 1.0 - beta_two**STEP

    def kernel(
        x_hbm, c_hbm, p_hbm, m_hbm, v_hbm,
        upd_out, basis_out, new_m, new_v,
        x, cot, proj, mom, sec,
        sfull, zsend, zrecv, exrecv, projd, grad,
        sibsend, sibrecv, own, cssend, csrecv, upd, basis,
        x_sem, l_sem, in_s, in_r, ex_s, ex_r, out_s, out_r,
        sib_s, sib_r, cs_s, cs_r, up_s, up_r, fw_s, fw_r,
        dn_s, dn_r, hi_s, hi_r,
    ):
        t = lax.axis_index("tensor")
        i = lax.axis_index("dp")
        n = tensor_count
        parity = lax.rem(i, 2)
        chip = lax.div(i, 2)
        sibling = i + 1 - 2 * parity
        lower = t < half
        tin = jnp.where(lower, t + 1, t - 1)
        tout = jnp.where(lower, t - 1, t + 1)
        dist = jnp.where(lower, half - 1 - t, t - half)
        is_ex = dist == 0
        has_outer = dist < half - 1
        lag = LAG + HOP_LAG * dist
        source = lax.div(i, ratio)
        part = lax.rem(i, ratio)

        def local(k, src, dst):
            return pltpu.make_async_copy(src, dst, l_sem.at[k])

        def xload(k):
            return pltpu.make_async_copy(
                x_hbm.at[pl.ds(k * tg, tg)], x.at[pl.ds(k * tg, tg)], x_sem.at[k]
            )

        loads = [
            local(0, p_hbm, proj),
            local(1, c_hbm, cot),
            local(2, m_hbm, mom),
            local(3, v_hbm, sec),
        ]
        loads[0].start()
        for k in range(K // GROUP):
            xload(k).start()
        for load in loads[1:]:
            load.start()

        barrier = pltpu.get_barrier_semaphore()

        @pl.when(t > 0)
        def _():
            pl.semaphore_signal(barrier, inc=1, device_id={"tensor": t - 1}, device_id_type=MESH)

        @pl.when(t < n - 1)
        def _():
            pl.semaphore_signal(barrier, inc=1, device_id={"tensor": t + 1}, device_id_type=MESH)

        pl.semaphore_signal(barrier, inc=1, device_id={"dp": sibling}, device_id_type=MESH)
        for d in range(1, m):
            peer = 2 * lax.rem(chip + d, m) + parity
            pl.semaphore_signal(barrier, inc=1, device_id={"dp": peer}, device_id_type=MESH)

        def remote(src, dst, send, recv, where):
            return pltpu.make_async_remote_copy(
                src_ref=src, dst_ref=dst, send_sem=send, recv_sem=recv,
                device_id=where, device_id_type=MESH,
            )

        def span(k):
            return pl.ds(pl.multiple_of(k * tc, tc), tc)

        def group(k):
            return pl.ds(pl.multiple_of(k * tg, tg), tg)

        def inward(k):
            return remote(zsend.at[span(k)], zrecv.at[span(k)], in_s.at[k], in_r.at[k], {"tensor": tin})

        def exchange(k):
            return remote(zsend.at[span(k)], exrecv.at[span(k)], ex_s.at[k], ex_r.at[k], {"tensor": tin})

        def outward(k):
            return remote(projd.at[span(k)], projd.at[span(k)], out_s.at[k], out_r.at[k], {"tensor": tout})

        def basis_down(k):
            return remote(basis.at[k], basis.at[k], dn_s.at[k], dn_r.at[k], {"tensor": t - 1})

        def basis_up(k):
            return remote(basis.at[k], basis.at[k], hi_s.at[k], hi_r.at[k], {"tensor": t + 1})

        def product(k):
            xload(k).wait()
            sfull[group(k)] = jnp.dot(
                x[group(k), :],
                proj[...],
                preferred_element_type=jnp.float32,
            )

        loads[0].wait()
        product(0)
        grad[...] = jnp.zeros_like(grad)
        pl.semaphore_wait(
            barrier, m + jnp.where(t > 0, 1, 0) + jnp.where(t < n - 1, 1, 0)
        )
        loads[1].wait()

        def reduce_step(k):
            @pl.when(has_outer)
            def _():
                inward(k).wait_recv()
                sfull[span(k)] = sfull[span(k)] + zrecv[span(k)].astype(jnp.float32)

            zsend[span(k)] = sfull[span(k)].astype(jnp.bfloat16)

            @pl.when(is_ex)
            def _():
                exchange(k).start()

            @pl.when(jnp.logical_not(is_ex))
            def _():
                inward(k).start()

        def total_step(k):
            @pl.when(is_ex)
            def _():
                exchange(k).wait_recv()
                projd[span(k)] = (
                    sfull[span(k)] + exrecv[span(k)].astype(jnp.float32)
                ).astype(jnp.bfloat16)

            @pl.when(jnp.logical_not(is_ex))
            def _():
                outward(k).wait_recv()

            @pl.when(has_outer)
            def _():
                outward(k).start()

            @pl.when(lax.rem(k, GROUP) == GROUP - 1)
            def _():
                tokens_now = group(lax.div(k, GROUP))

                def tile(q, carry):
                    cols = pl.ds(pl.multiple_of(q * w, w), w)
                    grad[:, cols] += lax.dot_general(
                        projd[tokens_now, :],
                        cot[tokens_now, cols],
                        (((0,), (0,)), ((), ())),
                        preferred_element_type=jnp.float32,
                    )
                    return carry

                lax.fori_loop(0, NC, tile, 0)

        def z_step(s, carry):
            @pl.when(jnp.logical_and(s + GROUP < K, lax.rem(s, GROUP) == 0))
            def _():
                product(lax.div(s, GROUP) + 1)

            @pl.when(s < K)
            def _():
                reduce_step(s)

            @pl.when(jnp.logical_and(s >= lag, s < lag + K))
            def _():
                total_step(s - lag)

            return carry

        lax.fori_loop(0, K + LAG + HOP_LAG * (half - 1), z_step, 0)

        @pl.when(t == source)
        def _():
            def send(k, carry):
                basis[k] = proj[pl.ds(pl.multiple_of(part * rows + k * br, br), br), :]

                @pl.when(t > 0)
                def _():
                    basis_down(k).start()

                @pl.when(t < n - 1)
                def _():
                    basis_up(k).start()

                return carry

            lax.fori_loop(0, NB, send, 0)

        def basis_step(k):
            @pl.when(t < source)
            def _():
                basis_down(k).wait_recv()

                @pl.when(t > 0)
                def _():
                    basis_down(k).start()

            @pl.when(t > source)
            def _():
                basis_up(k).wait_recv()

                @pl.when(t < n - 1)
                def _():
                    basis_up(k).start()

        def to_sibling(q):
            return remote(
                sibsend.at[q], sibrecv.at[q], sib_s.at[q], sib_r.at[q], {"dp": sibling}
            )

        def to_chip(q, d):
            peer = 2 * lax.rem(chip + d, m) + parity
            return remote(
                cssend.at[q, d], csrecv.at[q, d], cs_s.at[q, d], cs_r.at[q, d], {"dp": peer}
            )

        def block(owner):
            return pl.ds(pl.multiple_of(owner * r, r), r)

        def update_to_chip(q, d):
            peer = 2 * lax.rem(chip + d, m) + parity
            return remote(
                upd.at[q, block(i)], upd.at[q, block(i)], up_s.at[q, d], up_r.at[q, d],
                {"dp": peer},
            )

        def update_to_sibling(q, d):
            owner = 2 * lax.rem(chip - d + m, m) + parity
            return remote(
                upd.at[q, block(owner)], upd.at[q, block(owner)], fw_s.at[q, d], fw_r.at[q, d],
                {"dp": sibling},
            )

        def sibling_step(q, carry):
            cols = pl.ds(pl.multiple_of(q * w, w), w)
            for j in range(m):
                sibsend[q, j] = grad[block(2 * j + 1 - parity), cols].astype(jnp.bfloat16)
            to_sibling(q).start()
            return carry

        lax.fori_loop(0, NC, sibling_step, 0)

        def chip_step(q, carry):
            cols = pl.ds(pl.multiple_of(q * w, w), w)
            to_sibling(q).wait_recv()
            for d in range(1, m):
                j = lax.rem(chip + d, m)
                cssend[q, d] = (
                    grad[block(2 * j + parity), cols] + sibrecv[q, j].astype(jnp.float32)
                ).astype(jnp.bfloat16)
                to_chip(q, d).start()
            own[q] = grad[block(i), cols] + sibrecv[q, chip].astype(jnp.float32)
            return carry

        lax.fori_loop(0, NC, chip_step, 0)
        loads[2].wait()
        loads[3].wait()

        def adam_step(q, carry):
            cols = pl.ds(pl.multiple_of(q * w, w), w)

            @pl.when(q >= 1)
            def _():
                basis_step(q - 1)

            total = own[q]
            for d in range(1, m):
                to_chip(q, d).wait_recv()
                total = total + csrecv[q, d].astype(jnp.float32)
            gradient = total * scale
            moment = beta_one * mom[:, cols] + (1.0 - beta_one) * gradient
            second = beta_two * sec[:, cols] + (1.0 - beta_two) * gradient * gradient
            new_m[:, cols] = moment
            new_v[:, cols] = second
            upd[q, block(i)] = (
                moment / first_fix / (jnp.sqrt(second / second_fix) + epsilon)
            ).astype(jnp.bfloat16)
            for d in range(1, m):
                update_to_chip(q, d).start()
            update_to_sibling(q, 0).start()
            return carry

        lax.fori_loop(0, NC, adam_step, 0)

        def gather_step(q, carry):
            basis_step(q + NC - 1)
            for d in range(1, m):
                update_to_chip(q, d).wait_recv()
                update_to_sibling(q, d).start()
            return carry

        lax.fori_loop(0, NC, gather_step, 0)
        for k in range(2 * NC - 1, NB):
            basis_step(k)

        def sibling_wait(q, carry):
            for d in range(m):
                owner = 2 * lax.rem(chip - d + m, m) + 1 - parity
                remote(
                    upd.at[q, block(owner)], upd.at[q, block(owner)],
                    fw_s.at[q, d], fw_r.at[q, d], {"dp": sibling},
                ).wait_recv()
            return carry

        lax.fori_loop(0, NC, sibling_wait, 0)

        upd_copy = pltpu.make_async_copy(upd, upd_out, l_sem.at[0])
        upd_copy.start()
        basis_copy = pltpu.make_async_copy(basis, basis_out, l_sem.at[1])
        basis_copy.start()

        def drain_z(k, carry):
            @pl.when(is_ex)
            def _():
                exchange(k).wait_send()

            @pl.when(jnp.logical_not(is_ex))
            def _():
                inward(k).wait_send()

            @pl.when(has_outer)
            def _():
                outward(k).wait_send()

            return carry

        lax.fori_loop(0, K, drain_z, 0)

        def drain_basis(k, carry):
            @pl.when(jnp.logical_and(t <= source, t > 0))
            def _():
                basis_down(k).wait_send()

            @pl.when(jnp.logical_and(t >= source, t < n - 1))
            def _():
                basis_up(k).wait_send()

            return carry

        lax.fori_loop(0, NB, drain_basis, 0)

        def drain_dp(q, carry):
            to_sibling(q).wait_send()
            update_to_sibling(q, 0).wait_send()
            for d in range(1, m):
                to_chip(q, d).wait_send()
                update_to_chip(q, d).wait_send()
                update_to_sibling(q, d).wait_send()
            return carry

        lax.fori_loop(0, NC, drain_dp, 0)
        upd_copy.wait()
        basis_copy.wait()

    dma = pltpu.SemaphoreType.DMA
    bf16, f32 = jnp.bfloat16, jnp.float32
    scratch = [
        pltpu.VMEM((tokens, features), bf16),
        pltpu.VMEM((tokens, columns), bf16),
        pltpu.VMEM((features, rank), bf16),
        pltpu.VMEM((r, columns), f32),
        pltpu.VMEM((r, columns), f32),
        pltpu.VMEM((tokens, rank), f32),
        pltpu.VMEM((tokens, rank), bf16),
        pltpu.VMEM((tokens, rank), bf16),
        pltpu.VMEM((tokens, rank), bf16),
        pltpu.VMEM((tokens, rank), bf16),
        pltpu.VMEM((rank, columns), f32),
        pltpu.VMEM((NC, m, r, w), bf16),
        pltpu.VMEM((NC, m, r, w), bf16),
        pltpu.VMEM((NC, r, w), f32),
        pltpu.VMEM((NC, m, r, w), bf16),
        pltpu.VMEM((NC, m, r, w), bf16),
        pltpu.VMEM((NC, rank, w), bf16),
        pltpu.VMEM((NB, br, rank), bf16),
        dma((K // GROUP,)),
        dma((4,)),
        *[dma((K,))] * 6,
        *[dma((NC,))] * 2,
        *[dma((NC, m))] * 6,
        *[dma((NB,))] * 4,
    ]
    return kernel, scratch


def solution(mesh):
    tensor_count, data_count = mesh.shape["tensor"], mesh.shape["dp"]

    def on_device(inputs, cotangent, projector, weight, moment, second_moment):
        tokens, features = inputs.shape
        rank = projector.shape[1]
        rows, columns = weight.shape
        kernel, scratch = make_kernel(
            tensor_count, data_count, tokens, features, rank, rows, columns
        )
        any_space = pl.BlockSpec(memory_space=pl.ANY)
        in_vmem = pl.BlockSpec(memory_space=pltpu.VMEM)
        width, height = columns // COLUMN_CHUNKS, rows // BASIS_CHUNKS
        update, basis, moment, second_moment = pl.pallas_call(
            kernel,
            out_shape=(
                jax.ShapeDtypeStruct((COLUMN_CHUNKS, rank, width), jnp.bfloat16),
                jax.ShapeDtypeStruct((BASIS_CHUNKS, height, rank), jnp.bfloat16),
                jax.ShapeDtypeStruct(moment.shape, moment.dtype),
                jax.ShapeDtypeStruct(second_moment.shape, second_moment.dtype),
            ),
            in_specs=[any_space] * 5,
            out_specs=(any_space, any_space, in_vmem, in_vmem),
            scratch_shapes=scratch,
            compiler_params=pltpu.CompilerParams(
                collective_id=0, has_side_effects=True, vmem_limit_bytes=60 * 1024 * 1024
            ),
        )(inputs, cotangent, projector, moment, second_moment)
        basis = basis.reshape(rows, rank)
        tiles = 4
        line = rows // tiles

        def finish(w_ref, b_ref, u_ref, m_ref, v_ref, out_ref, m_out, v_out):
            for q in range(COLUMN_CHUNKS):
                cols = slice(q * width, (q + 1) * width)
                expanded = jnp.dot(b_ref[...], u_ref[q], preferred_element_type=jnp.float32)
                out_ref[:, cols] = (
                    w_ref[:, cols].astype(jnp.float32) - step_size * expanded
                ).astype(jnp.bfloat16)

            @pl.when(pl.program_id(0) == 0)
            def _():
                m_out[...] = m_ref[...]
                v_out[...] = v_ref[...]

        state = pl.BlockSpec(moment.shape, lambda k: (0, 0))
        tile = pl.BlockSpec((line, columns), lambda k: (k, 0))
        return pl.pallas_call(
            finish,
            grid=(tiles,),
            out_shape=(
                jax.ShapeDtypeStruct(weight.shape, weight.dtype),
                jax.ShapeDtypeStruct(moment.shape, moment.dtype),
                jax.ShapeDtypeStruct(second_moment.shape, second_moment.dtype),
            ),
            in_specs=[
                tile,
                pl.BlockSpec((line, rank), lambda k: (k, 0)),
                pl.BlockSpec(update.shape, lambda k: (0, 0, 0)),
                state,
                state,
            ],
            out_specs=(tile, state, state),
            compiler_params=pltpu.CompilerParams(vmem_limit_bytes=60 * 1024 * 1024),
        )(weight, basis, update, moment, second_moment)

    return jax.shard_map(
        on_device,
        mesh=mesh,
        in_specs=(
            P("dp", "tensor"),
            P("dp", "tensor"),
            P("tensor", None),
            P("dp", "tensor"),
            P("dp", "tensor"),
            P("dp", "tensor"),
        ),
        out_specs=(P("dp", "tensor"), P("dp", "tensor"), P("dp", "tensor")),
        check_vma=False,
    )
```

```python
import math

import jax
import jax.numpy as jnp
from jax import lax
from jax.experimental import pallas as pl
from jax.experimental.pallas import tpu as pltpu
from jax.sharding import PartitionSpec as P

STEP = 1000

beta_one = 0.9
beta_two = 0.999
epsilon = 1e-08
step_size = 0.5

TOKEN_CHUNKS = 16
GROUP = 2
LAG = 3
HOP_LAG = 7
COLUMN_CHUNKS = 4
BASIS_CHUNKS = 8
MESH = pl.DeviceIdType.MESH


def make_kernel(tensor_count, data_count, tokens, features, rank, rows, columns):
    K, NC, NB = TOKEN_CHUNKS, COLUMN_CHUNKS, BASIS_CHUNKS
    tc, w, br = tokens // K, columns // NC, rows // NB
    tg = tc * GROUP
    r = rank // data_count
    m = data_count // 2
    half = tensor_count // 2
    ratio = features // rows
    scale = 1.0 / math.sqrt(tokens * data_count)
    first_fix = 1.0 - beta_one**STEP
    second_fix = 1.0 - beta_two**STEP

    def kernel(
        x_hbm, c_hbm, p_hbm, m_hbm, v_hbm,
        upd_out, basis_out, new_m, new_v,
        x, cot, proj, mom, sec,
        sfull, zsend, zrecv, exrecv, projd, grad,
        sibsend, sibrecv, own, cssend, csrecv, upd, basis,
        x_sem, l_sem, in_s, in_r, ex_s, ex_r, out_s, out_r,
        sib_s, sib_r, cs_s, cs_r, up_s, up_r, fw_s, fw_r,
        dn_s, dn_r, hi_s, hi_r,
    ):
        t = lax.axis_index("tensor")
        i = lax.axis_index("dp")
        n = tensor_count
        parity = lax.rem(i, 2)
        chip = lax.div(i, 2)
        sibling = i + 1 - 2 * parity
        lower = t < half
        tin = jnp.where(lower, t + 1, t - 1)
        tout = jnp.where(lower, t - 1, t + 1)
        dist = jnp.where(lower, half - 1 - t, t - half)
        is_ex = dist == 0
        has_outer = dist < half - 1
        lag = LAG + HOP_LAG * dist
        source = lax.div(i, ratio)
        part = lax.rem(i, ratio)

        def local(k, src, dst):
            return pltpu.make_async_copy(src, dst, l_sem.at[k])

        def xload(k):
            return pltpu.make_async_copy(
                x_hbm.at[pl.ds(k * tg, tg)], x.at[pl.ds(k * tg, tg)], x_sem.at[k]
            )

        loads = [
            local(0, p_hbm, proj),
            local(1, c_hbm, cot),
            local(2, m_hbm, mom),
            local(3, v_hbm, sec),
        ]
        loads[0].start()
        for k in range(K // GROUP):
            xload(k).start()
        for load in loads[1:]:
            load.start()

        barrier = pltpu.get_barrier_semaphore()

        @pl.when(t > 0)
        def _():
            pl.semaphore_signal(barrier, inc=1, device_id={"tensor": t - 1}, device_id_type=MESH)

        @pl.when(t < n - 1)
        def _():
            pl.semaphore_signal(barrier, inc=1, device_id={"tensor": t + 1}, device_id_type=MESH)

        pl.semaphore_signal(barrier, inc=1, device_id={"dp": sibling}, device_id_type=MESH)
        for d in range(1, m):
            peer = 2 * lax.rem(chip + d, m) + parity
            pl.semaphore_signal(barrier, inc=1, device_id={"dp": peer}, device_id_type=MESH)

        def remote(src, dst, send, recv, where):
            return pltpu.make_async_remote_copy(
                src_ref=src, dst_ref=dst, send_sem=send, recv_sem=recv,
                device_id=where, device_id_type=MESH,
            )

        def span(k):
            return pl.ds(pl.multiple_of(k * tc, tc), tc)

        def group(k):
            return pl.ds(pl.multiple_of(k * tg, tg), tg)

        def inward(k):
            return remote(zsend.at[span(k)], zrecv.at[span(k)], in_s.at[k], in_r.at[k], {"tensor": tin})

        def exchange(k):
            return remote(zsend.at[span(k)], exrecv.at[span(k)], ex_s.at[k], ex_r.at[k], {"tensor": tin})

        def outward(k):
            return remote(projd.at[span(k)], projd.at[span(k)], out_s.at[k], out_r.at[k], {"tensor": tout})

        def basis_down(k):
            return remote(basis.at[k], basis.at[k], dn_s.at[k], dn_r.at[k], {"tensor": t - 1})

        def basis_up(k):
            return remote(basis.at[k], basis.at[k], hi_s.at[k], hi_r.at[k], {"tensor": t + 1})

        def product(k):
            xload(k).wait()
            sfull[group(k)] = jnp.dot(
                x[group(k), :],
                proj[...],
                preferred_element_type=jnp.float32,
            )

        loads[0].wait()
        product(0)
        grad[...] = jnp.zeros_like(grad)
        pl.semaphore_wait(
            barrier, m + jnp.where(t > 0, 1, 0) + jnp.where(t < n - 1, 1, 0)
        )
        loads[1].wait()

        def reduce_step(k):
            @pl.when(has_outer)
            def _():
                inward(k).wait_recv()
                sfull[span(k)] = sfull[span(k)] + zrecv[span(k)].astype(jnp.float32)

            zsend[span(k)] = sfull[span(k)].astype(jnp.bfloat16)

            @pl.when(is_ex)
            def _():
                exchange(k).start()

            @pl.when(jnp.logical_not(is_ex))
            def _():
                inward(k).start()

        def total_step(k):
            @pl.when(is_ex)
            def _():
                exchange(k).wait_recv()
                projd[span(k)] = (
                    sfull[span(k)] + exrecv[span(k)].astype(jnp.float32)
                ).astype(jnp.bfloat16)

            @pl.when(jnp.logical_not(is_ex))
            def _():
                outward(k).wait_recv()

            @pl.when(has_outer)
            def _():
                outward(k).start()

            @pl.when(lax.rem(k, GROUP) == GROUP - 1)
            def _():
                tokens_now = group(lax.div(k, GROUP))

                def tile(q, carry):
                    cols = pl.ds(pl.multiple_of(q * w, w), w)
                    grad[:, cols] += lax.dot_general(
                        projd[tokens_now, :],
                        cot[tokens_now, cols],
                        (((0,), (0,)), ((), ())),
                        preferred_element_type=jnp.float32,
                    )
                    return carry

                lax.fori_loop(0, NC, tile, 0)

        def send_basis():
            def send(k, carry):
                basis[k] = proj[pl.ds(pl.multiple_of(part * rows + k * br, br), br), :]

                @pl.when(t > 0)
                def _():
                    basis_down(k).start()

                @pl.when(t < n - 1)
                def _():
                    basis_up(k).start()

                return carry

            lax.fori_loop(0, NB, send, 0)

        is_source = t == source

        def z_step(s, carry):
            @pl.when(jnp.logical_and(s + GROUP < K, lax.rem(s, GROUP) == 0))
            def _():
                product(lax.div(s, GROUP) + 1)

            @pl.when(s < K)
            def _():
                reduce_step(s)

            @pl.when(jnp.logical_and(is_source, s == jnp.where(has_outer, lag + K, K)))
            def _():
                send_basis()

            @pl.when(jnp.logical_and(s >= lag, s < lag + K))
            def _():
                total_step(s - lag)

            return carry

        lax.fori_loop(0, K + LAG + HOP_LAG * (half - 1) + 1, z_step, 0)

        def basis_step(k):
            @pl.when(t < source)
            def _():
                basis_down(k).wait_recv()

                @pl.when(t > 0)
                def _():
                    basis_down(k).start()

            @pl.when(t > source)
            def _():
                basis_up(k).wait_recv()

                @pl.when(t < n - 1)
                def _():
                    basis_up(k).start()

        def to_sibling(q):
            return remote(
                sibsend.at[q], sibrecv.at[q], sib_s.at[q], sib_r.at[q], {"dp": sibling}
            )

        def to_chip(q, d):
            peer = 2 * lax.rem(chip + d, m) + parity
            return remote(
                cssend.at[q, d], csrecv.at[q, d], cs_s.at[q, d], cs_r.at[q, d], {"dp": peer}
            )

        def block(owner):
            return pl.ds(pl.multiple_of(owner * r, r), r)

        def update_to_chip(q, d):
            peer = 2 * lax.rem(chip + d, m) + parity
            return remote(
                upd.at[q, block(i)], upd.at[q, block(i)], up_s.at[q, d], up_r.at[q, d],
                {"dp": peer},
            )

        def update_to_sibling(q, d):
            owner = 2 * lax.rem(chip - d + m, m) + parity
            return remote(
                upd.at[q, block(owner)], upd.at[q, block(owner)], fw_s.at[q, d], fw_r.at[q, d],
                {"dp": sibling},
            )

        def sibling_step(q, carry):
            cols = pl.ds(pl.multiple_of(q * w, w), w)
            for j in range(m):
                sibsend[q, j] = grad[block(2 * j + 1 - parity), cols].astype(jnp.bfloat16)
            to_sibling(q).start()
            return carry

        lax.fori_loop(0, NC, sibling_step, 0)

        def chip_step(q, carry):
            cols = pl.ds(pl.multiple_of(q * w, w), w)
            to_sibling(q).wait_recv()
            for d in range(1, m):
                j = lax.rem(chip + d, m)
                cssend[q, d] = (
                    grad[block(2 * j + parity), cols] + sibrecv[q, j].astype(jnp.float32)
                ).astype(jnp.bfloat16)
                to_chip(q, d).start()
            own[q] = grad[block(i), cols] + sibrecv[q, chip].astype(jnp.float32)
            return carry

        lax.fori_loop(0, NC, chip_step, 0)
        loads[2].wait()
        loads[3].wait()

        def adam_step(q, carry):
            cols = pl.ds(pl.multiple_of(q * w, w), w)

            basis_step(q)

            total = own[q]
            for d in range(1, m):
                to_chip(q, d).wait_recv()
                total = total + csrecv[q, d].astype(jnp.float32)
            gradient = total * scale
            moment = beta_one * mom[:, cols] + (1.0 - beta_one) * gradient
            second = beta_two * sec[:, cols] + (1.0 - beta_two) * gradient * gradient
            new_m[:, cols] = moment
            new_v[:, cols] = second
            upd[q, block(i)] = (
                moment / first_fix / (jnp.sqrt(second / second_fix) + epsilon)
            ).astype(jnp.bfloat16)
            for d in range(1, m):
                update_to_chip(q, d).start()
            update_to_sibling(q, 0).start()
            return carry

        lax.fori_loop(0, NC, adam_step, 0)

        def gather_step(q, carry):
            basis_step(q + NC)
            for d in range(1, m):
                update_to_chip(q, d).wait_recv()
                update_to_sibling(q, d).start()
            return carry

        lax.fori_loop(0, NC, gather_step, 0)
        for k in range(2 * NC, NB):
            basis_step(k)

        def sibling_wait(q, carry):
            for d in range(m):
                owner = 2 * lax.rem(chip - d + m, m) + 1 - parity
                remote(
                    upd.at[q, block(owner)], upd.at[q, block(owner)],
                    fw_s.at[q, d], fw_r.at[q, d], {"dp": sibling},
                ).wait_recv()
            return carry

        lax.fori_loop(0, NC, sibling_wait, 0)

        upd_copy = pltpu.make_async_copy(upd, upd_out, l_sem.at[0])
        upd_copy.start()
        basis_copy = pltpu.make_async_copy(basis, basis_out, l_sem.at[1])
        basis_copy.start()

        def drain_z(k, carry):
            @pl.when(is_ex)
            def _():
                exchange(k).wait_send()

            @pl.when(jnp.logical_not(is_ex))
            def _():
                inward(k).wait_send()

            @pl.when(has_outer)
            def _():
                outward(k).wait_send()

            return carry

        lax.fori_loop(0, K, drain_z, 0)

        def drain_basis(k, carry):
            @pl.when(jnp.logical_and(t <= source, t > 0))
            def _():
                basis_down(k).wait_send()

            @pl.when(jnp.logical_and(t >= source, t < n - 1))
            def _():
                basis_up(k).wait_send()

            return carry

        lax.fori_loop(0, NB, drain_basis, 0)

        def drain_dp(q, carry):
            to_sibling(q).wait_send()
            update_to_sibling(q, 0).wait_send()
            for d in range(1, m):
                to_chip(q, d).wait_send()
                update_to_chip(q, d).wait_send()
                update_to_sibling(q, d).wait_send()
            return carry

        lax.fori_loop(0, NC, drain_dp, 0)
        upd_copy.wait()
        basis_copy.wait()

    dma = pltpu.SemaphoreType.DMA
    bf16, f32 = jnp.bfloat16, jnp.float32
    scratch = [
        pltpu.VMEM((tokens, features), bf16),
        pltpu.VMEM((tokens, columns), bf16),
        pltpu.VMEM((features, rank), bf16),
        pltpu.VMEM((r, columns), f32),
        pltpu.VMEM((r, columns), f32),
        pltpu.VMEM((tokens, rank), f32),
        pltpu.VMEM((tokens, rank), bf16),
        pltpu.VMEM((tokens, rank), bf16),
        pltpu.VMEM((tokens, rank), bf16),
        pltpu.VMEM((tokens, rank), bf16),
        pltpu.VMEM((rank, columns), f32),
        pltpu.VMEM((NC, m, r, w), bf16),
        pltpu.VMEM((NC, m, r, w), bf16),
        pltpu.VMEM((NC, r, w), f32),
        pltpu.VMEM((NC, m, r, w), bf16),
        pltpu.VMEM((NC, m, r, w), bf16),
        pltpu.VMEM((NC, rank, w), bf16),
        pltpu.VMEM((NB, br, rank), bf16),
        dma((K // GROUP,)),
        dma((4,)),
        *[dma((K,))] * 6,
        *[dma((NC,))] * 2,
        *[dma((NC, m))] * 6,
        *[dma((NB,))] * 4,
    ]
    return kernel, scratch


def solution(mesh):
    tensor_count, data_count = mesh.shape["tensor"], mesh.shape["dp"]

    def on_device(inputs, cotangent, projector, weight, moment, second_moment):
        tokens, features = inputs.shape
        rank = projector.shape[1]
        rows, columns = weight.shape
        kernel, scratch = make_kernel(
            tensor_count, data_count, tokens, features, rank, rows, columns
        )
        any_space = pl.BlockSpec(memory_space=pl.ANY)
        in_vmem = pl.BlockSpec(memory_space=pltpu.VMEM)
        width, height = columns // COLUMN_CHUNKS, rows // BASIS_CHUNKS
        update, basis, moment, second_moment = pl.pallas_call(
            kernel,
            out_shape=(
                jax.ShapeDtypeStruct((COLUMN_CHUNKS, rank, width), jnp.bfloat16),
                jax.ShapeDtypeStruct((BASIS_CHUNKS, height, rank), jnp.bfloat16),
                jax.ShapeDtypeStruct(moment.shape, moment.dtype),
                jax.ShapeDtypeStruct(second_moment.shape, second_moment.dtype),
            ),
            in_specs=[any_space] * 5,
            out_specs=(any_space, any_space, in_vmem, in_vmem),
            scratch_shapes=scratch,
            compiler_params=pltpu.CompilerParams(
                collective_id=0, has_side_effects=True, vmem_limit_bytes=60 * 1024 * 1024
            ),
        )(inputs, cotangent, projector, moment, second_moment)
        basis = basis.reshape(rows, rank)
        tiles = 4
        line = rows // tiles

        def finish(w_ref, b_ref, u_ref, m_ref, v_ref, out_ref, m_out, v_out):
            for q in range(COLUMN_CHUNKS):
                cols = slice(q * width, (q + 1) * width)
                expanded = jnp.dot(b_ref[...], u_ref[q], preferred_element_type=jnp.float32)
                out_ref[:, cols] = (
                    w_ref[:, cols].astype(jnp.float32) - step_size * expanded
                ).astype(jnp.bfloat16)

            @pl.when(pl.program_id(0) == 0)
            def _():
                m_out[...] = m_ref[...]
                v_out[...] = v_ref[...]

        state = pl.BlockSpec(moment.shape, lambda k: (0, 0))
        tile = pl.BlockSpec((line, columns), lambda k: (k, 0))
        return pl.pallas_call(
            finish,
            grid=(tiles,),
            out_shape=(
                jax.ShapeDtypeStruct(weight.shape, weight.dtype),
                jax.ShapeDtypeStruct(moment.shape, moment.dtype),
                jax.ShapeDtypeStruct(second_moment.shape, second_moment.dtype),
            ),
            in_specs=[
                tile,
                pl.BlockSpec((line, rank), lambda k: (k, 0)),
                pl.BlockSpec(update.shape, lambda k: (0, 0, 0)),
                state,
                state,
            ],
            out_specs=(tile, state, state),
            compiler_params=pltpu.CompilerParams(vmem_limit_bytes=60 * 1024 * 1024),
        )(weight, basis, update, moment, second_moment)

    return jax.shard_map(
        on_device,
        mesh=mesh,
        in_specs=(
            P("dp", "tensor"),
            P("dp", "tensor"),
            P("tensor", None),
            P("dp", "tensor"),
            P("dp", "tensor"),
            P("dp", "tensor"),
        ),
        out_specs=(P("dp", "tensor"), P("dp", "tensor"), P("dp", "tensor")),
        check_vma=False,
    )
```
